512 devices in a mesh: lon: 32 (over z_lo, x, core), lat: 16 (over y, z_hi).
Axes of the slice: x: 4, y: 8, z: 8 (z_hi: 2, z_lo: 4; z = z_hi * 4 + z_lo), core: 2. Of those that a mesh axis runs over, the one named last changes fastest.
Arguments:
- fields: bfloat16 [768, 1536, 128], P('lat', 'lon'), may hold values from -6 to 6
- cotangent: bfloat16 [768, 1536, 128], P('lat', 'lon'), may hold values from -6 to 6
- mixing: bfloat16 [9, 128, 128], replicated, may hold values from -0.1875 to 0.1875
- widths: int32 [768, 5], replicated, may hold values from 1 to 16, as said below
Outputs:
- features_out: bfloat16 [768, 1536, 128], P('lat', 'lon')
- grad_input: bfloat16 [768, 1536, 128], P('lat', 'lon')
The draws below stay inside these ranges and needn't reach their ends.
Inputs may be any that keep to these rules, and one draw needn't show every extreme that they name: `widths`: rows 0 and 767 have 16 at every row offset.
All inputs are finite; a program needn't handle non-finite values.
Results may differ from the reference program's by a relative error of at most 0.006.
Values may be sent and summed in bfloat16 or wider, within the bound.
A program may use at most 64 MiB of HBM per device.

```python
import jax
import jax.numpy as jnp
from jax import lax

CH = 128
BASIS = 9
RAD = 2
HALO = 16
NLAT = 768
NLON = 1536


def draw_widths(key, part):
    key = jax.random.fold_in(key, 7)
    row_index = jnp.arange(NLAT, dtype=jnp.int32)
    pole_gap = jnp.minimum(row_index, NLAT - 1 - row_index)
    scale_rows = max(NLAT // 16, 1)
    base_width = HALO * scale_rows // (pole_gap + scale_rows)
    jitter = jax.random.randint(key, (NLAT, 2 * RAD + 1), -1, 2)
    width_rows = jnp.clip(base_width[:, None] + jitter, 1, HALO)
    return jnp.where(pole_gap[:, None] == 0, HALO, width_rows).astype(jnp.int32)


def level_of(key, dims, cuts, smallest, top_value):
    def one(position, blocks):
        steps = jax.random.uniform(jax.random.fold_in(jax.random.fold_in(key, 6), position), (blocks,), jnp.float32, smallest / len(cuts), top_value / len(cuts))
        return jnp.repeat(jnp.exp(steps), dims[position] // blocks).reshape((-1,) + (1,) * (len(dims) - position - 1))

    factor_of = one(*cuts[0])
    for cut in cuts[1:]:
        factor_of = factor_of * one(*cut)
    return factor_of


def gaussian(rng, shape, width, reach, cuts=(), kind=jnp.bfloat16):
    result = width * jax.random.normal(rng, shape, jnp.float32)
    if cuts:
        result = result * level_of(rng, shape, cuts, -0.22, 0.18)
    return jnp.clip(result, -reach, reach).astype(kind)


def setup_inputs(seed: int = 0) -> dict:
    splits = jax.random.split(jax.random.key(seed), 5)
    return {
        "fields": gaussian(splits[0], (NLAT, NLON, CH), 1.0, 6.0, ((0, 16), (1, 32))),
        "cotangent": gaussian(splits[1], (NLAT, NLON, CH), 1.0, 6.0, ((0, 16), (1, 32))),
        "mixing": gaussian(splits[2], (BASIS, CH, CH), (BASIS * CH) ** -0.5, 0.1875),
        "widths": draw_widths(jax.random.fold_in(splits[4], 71), 0),
    }


centers = (-0.5, 0.0, 0.5)


def basis_table(widths, radius, halo_cols):
    offset = jnp.arange(2 * halo_cols + 1, dtype=jnp.float32) - halo_cols
    foot_width = widths.astype(jnp.float32)[:, :, None]
    along_lon = offset[None, None, :] / (foot_width + 1.0)
    across = (jnp.arange(2 * radius + 1, dtype=jnp.float32) - radius) / (radius + 1.0)
    inside = jnp.abs(offset)[None, None, :] <= foot_width
    weight_norm = 3.0 / (2.0 * foot_width + 1.0)
    pieces = []
    for lon_center in centers:
        hat_along = jnp.maximum(0.0, 1.0 - 2.0 * jnp.abs(along_lon - lon_center))
        for lat_center in centers:
            hat_across = jnp.maximum(0.0, 1.0 - 2.0 * jnp.abs(across - lat_center))
            pieces.append(jnp.where(inside, hat_along * hat_across[None, :, None] * weight_norm, 0.0))
    return jnp.stack(pieces, axis=1)


def rounded(values):
    return lax.optimization_barrier(values.astype(jnp.bfloat16)).astype(jnp.float32)


def reference(fields, cotangent, mixing, widths):
    radius = RAD
    halo_cols = HALO
    row_span = 2 * radius + 1
    coeffs = rounded(basis_table(widths, radius, halo_cols))
    mixing_f32 = mixing.astype(jnp.float32)

    wrapped = jnp.concatenate((fields[:, NLON - halo_cols:], fields, fields[:, :halo_cols]), axis=1)
    wrapped = jnp.pad(wrapped, ((radius, radius), (0, 0), (0, 0)))

    def forward_row(row_id):
        window = lax.dynamic_slice_in_dim(wrapped, row_id, row_span, 0).astype(jnp.float32)
        operand = jnp.transpose(window, (2, 0, 1))
        kernel = lax.dynamic_index_in_dim(coeffs, row_id, 0, keepdims=False)
        convolved = lax.conv_general_dilated(operand, kernel, (1,), "VALID", dimension_numbers=("NCH", "OIH", "NCH"), precision=lax.Precision.HIGHEST)
        basis_out = rounded(convolved)
        return jnp.einsum("ckj,kcd->jd", basis_out, mixing_f32, precision=lax.Precision.HIGHEST).astype(jnp.bfloat16)

    features_out = lax.map(forward_row, jnp.arange(NLAT, dtype=jnp.int32))

    cot_wide = jnp.concatenate((cotangent[:, NLON - halo_cols:], cotangent, cotangent[:, :halo_cols]), axis=1)
    cot_wide = jnp.pad(cot_wide, ((radius, radius), (0, 0), (0, 0)))
    table_pad = jnp.pad(coeffs, ((radius, radius), (0, 0), (0, 0), (0, 0)))

    def mixed_row(row_id):
        cot_line = lax.dynamic_index_in_dim(cot_wide, row_id, 0, keepdims=False).astype(jnp.float32)
        return rounded(jnp.einsum("jd,kcd->kjc", cot_line, mixing_f32, precision=lax.Precision.HIGHEST))

    carried = jnp.stack([mixed_row(jnp.int32(number)) for number in range(2 * radius)]).astype(jnp.float32)

    def adjoint_row(carried, row_id):
        new_rows = mixed_row(row_id + 2 * radius)
        window = jnp.concatenate((carried, new_rows[None]), axis=0)
        sources = jnp.stack([window[2 * radius - offset_row] for offset_row in range(row_span)], axis=0)
        operand = jnp.transpose(sources, (3, 0, 1, 2)).reshape(sources.shape[3], row_span * sources.shape[1], sources.shape[2])
        kernel = jnp.stack([lax.dynamic_index_in_dim(table_pad, row_id + 2 * radius - offset_row, 0, keepdims=False)[:, offset_row, ::-1] for offset_row in range(row_span)], axis=0)
        kernel = kernel.reshape(1, row_span * kernel.shape[1], kernel.shape[2])
        convolved = lax.conv_general_dilated(operand, kernel, (1,), "VALID", dimension_numbers=("NCH", "OIH", "NCH"), precision=lax.Precision.HIGHEST)
        return window[1:], jnp.transpose(convolved[:, 0, :]).astype(jnp.bfloat16)

    carried, grad_input = lax.scan(adjoint_row, carried, jnp.arange(NLAT, dtype=jnp.int32))
    return features_out, grad_input
```

```python
import functools

import jax
import jax.numpy as jnp
from jax import lax
from jax.experimental import pallas as pl
from jax.experimental.pallas import tpu as pltpu
from jax.sharding import PartitionSpec as P

RAD = 2
HALO = 16
SPAN = 2 * RAD + 1
BLOCK = 16
REACH = BLOCK + 2 * HALO
TAPS = 256
CENTERS = (-0.5, 0.0, 0.5)


def padded_2(cells, sides, width, closed):
    for axis, dim in sides:
        count = lax.axis_size(axis)
        ends = count if closed else count - 1
        head = lax.slice_in_dim(cells, 0, width, axis=dim)
        tail = lax.slice_in_dim(cells, cells.shape[dim] - width, cells.shape[dim], axis=dim)
        cells = jnp.concatenate(
            [
                lax.ppermute(tail, axis, [(i, (i + 1) % count) for i in range(ends)]),
                cells,
                lax.ppermute(head, axis, [((i + 1) % count, i) for i in range(ends)]),
            ],
            axis=dim,
        )
    return cells


def widths_by_tap(widths, local, wide):
    rows = wide.shape[1]
    total = widths.shape[0]
    first = lax.axis_index("lat") * rows
    start = jnp.clip(first - 8, 0, total - rows - 16)
    start = pl.multiple_of(start, 8)
    local[...] = jnp.zeros_like(local)
    local[pl.ds(pl.multiple_of(start - first + 16, 8), rows + 16), :] = widths[
        pl.ds(start, rows + 16), :
    ].astype(jnp.float32)
    source = lax.broadcasted_iota(jnp.int32, (SPAN, TAPS), 0)
    tap_row = lax.broadcasted_iota(jnp.int32, (SPAN, TAPS), 1) // REACH
    own = (source == tap_row).astype(jnp.bfloat16)
    dot = functools.partial(jnp.dot, preferred_element_type=jnp.float32)
    wide[0] = dot(local[16 : 16 + rows, :].astype(jnp.bfloat16), own)
    turned = jnp.zeros((rows, TAPS), jnp.float32)
    for r in range(SPAN):
        pick = ((source == SPAN - 1 - r) & (tap_row == r)).astype(jnp.bfloat16)
        turned += dot(local[16 + r - RAD : 16 + r - RAD + rows, :].astype(jnp.bfloat16), pick)
    wide[1] = turned


def taps(foot_width):
    lane = lax.broadcasted_iota(jnp.int32, (BLOCK, TAPS), 1)
    tap_row = lane // REACH
    offset = (
        lane - tap_row * REACH - lax.broadcasted_iota(jnp.int32, (BLOCK, TAPS), 0) - HALO
    ).astype(jnp.float32)
    across = (tap_row[:1].astype(jnp.float32) - RAD) / (RAD + 1.0)
    norm = 3.0 / (2.0 * foot_width + 1.0)
    inside = jnp.abs(offset) <= foot_width
    along = offset * (1.0 / (foot_width + 1.0))
    pieces = []
    scales = [norm * jnp.maximum(0.0, 1.0 - 2.0 * jnp.abs(across - c)) for c in CENTERS]
    for lon_center in CENTERS:
        hat = jnp.maximum(0.0, 1.0 - 2.0 * jnp.abs(along - lon_center))
        hat = jnp.where(inside, hat, 0.0)
        pieces += [(hat * scale).astype(jnp.bfloat16) for scale in scales]
    return jnp.concatenate(pieces, axis=0)


def kernel(cells, mixing, widths, features, gradient, local, wide, basis, turned):
    rows, columns, channels = features.shape
    count = mixing.shape[0]
    blocks = columns // BLOCK
    group = basis.shape[0] // columns
    widths_by_tap(widths, local, wide)
    for k in range(count):
        turned[0, k * channels : (k + 1) * channels, :] = mixing[k]
        turned[1, k * channels : (k + 1) * channels, :] = (
            mixing[count - 1 - k].astype(jnp.float32).T.astype(jnp.bfloat16)
        )
    for side, result in enumerate((features, gradient)):

        def rows_of(step, carry, side=side, result=result):
            def one_row(slot, carry):
                row = step * group + slot
                coeffs = taps(wide[side, pl.ds(row, 1), :])
                data = jnp.concatenate(
                    [
                        jnp.concatenate(
                            [
                                cells[side, row + r, BLOCK * b : BLOCK * b + REACH, :]
                                for r in range(SPAN)
                            ]
                            + [cells[side, row, :TAPS - SPAN * REACH, :]],
                            axis=0,
                        )
                        for b in range(blocks)
                    ],
                    axis=1,
                )
                out = jnp.dot(coeffs, data, preferred_element_type=jnp.float32).astype(jnp.bfloat16)
                for b in range(blocks):
                    for k in range(count):
                        basis[
                            pl.ds(pl.multiple_of(slot * columns + BLOCK * b, BLOCK), BLOCK),
                            k * channels : (k + 1) * channels,
                        ] = out[k * BLOCK : (k + 1) * BLOCK, b * channels : (b + 1) * channels]
                return carry

            lax.fori_loop(0, group, one_row, 0)
            mixed = jnp.dot(basis[...], turned[side], preferred_element_type=jnp.float32)
            result[pl.ds(step * group, group)] = mixed.astype(jnp.bfloat16).reshape(
                group, columns, channels
            )
            return carry

        lax.fori_loop(0, rows // group, rows_of, 0)


def body(fields, cotangent, mixing, widths):
    rows, columns, channels = fields.shape
    count = mixing.shape[0]
    group = 8
    cells = jnp.stack([fields, cotangent])
    cells = padded_2(cells, (("lat", 1),), RAD, False)
    cells = padded_2(cells, (("lon", 2),), HALO, True)
    shape = jax.ShapeDtypeStruct(fields.shape, jnp.bfloat16)
    vmem = pl.BlockSpec(memory_space=pltpu.VMEM)
    return pl.pallas_call(
        kernel,
        out_shape=(shape, shape),
        in_specs=[vmem] * 3,
        out_specs=(vmem, vmem),
        scratch_shapes=[
            pltpu.VMEM((rows + 32, SPAN), jnp.float32),
            pltpu.VMEM((2, rows, TAPS), jnp.float32),
            pltpu.VMEM((group * columns, count * channels), jnp.bfloat16),
            pltpu.VMEM((2, count * channels, channels), jnp.bfloat16),
        ],
        compiler_params=pltpu.CompilerParams(vmem_limit_bytes=48 * 1024 * 1024),
    )(cells, mixing, widths)


def solution(mesh):
    in_specs = (P("lat", "lon", None), P("lat", "lon", None), P(), P())
    out_specs = (P("lat", "lon", None), P("lat", "lon", None))
    return jax.shard_map(body, mesh=mesh, in_specs=in_specs, out_specs=out_specs, check_vma=False)
```

```python
import functools

import jax
import jax.numpy as jnp
from jax import lax
from jax.experimental import pallas as pl
from jax.experimental.pallas import tpu as pltpu
from jax.sharding import PartitionSpec as P

RAD = 2
HALO = 16
SPAN = 2 * RAD + 1
BLOCK = 16
REACH = BLOCK + 2 * HALO
TAPS = 256
CENTERS = (-0.5, 0.0, 0.5)


def widths_by_tap(widths, straight, turned, wide):
    rows = wide.shape[1]
    total = widths.shape[1]
    first = pl.multiple_of(lax.axis_index("lat") * rows, 8)
    source = lax.broadcasted_iota(jnp.int32, (SPAN, TAPS), 0)
    tap_row = lax.broadcasted_iota(jnp.int32, (SPAN, TAPS), 1) // REACH
    values = widths[...].astype(jnp.float32).astype(jnp.bfloat16)
    for pick, table in ((source == tap_row, straight), (source == SPAN - 1 - tap_row, turned)):
        table[:8] = jnp.zeros((8, TAPS), jnp.float32)
        table[total + 8 :] = jnp.zeros((8, TAPS), jnp.float32)
        table[8 : total + 8] = lax.dot_general(
            values,
            pick.astype(jnp.bfloat16),
            (((0,), (0,)), ((), ())),
            preferred_element_type=jnp.float32,
        )
    tap_row = lax.broadcasted_iota(jnp.int32, (rows, TAPS), 1) // REACH
    read = first + lax.broadcasted_iota(jnp.int32, (rows, TAPS), 0) + tap_row - RAD
    on_grid = (read >= 0) & (read < total)
    wide[0] = jnp.where(on_grid, straight[pl.ds(first + 8, rows), :], -2.0)
    near = turned[pl.ds(first, rows + 16), :]
    value = near[8 - RAD : 8 - RAD + rows]
    for r in range(1, SPAN):
        value = jnp.where(tap_row == r, near[8 - RAD + r : 8 - RAD + r + rows], value)
    wide[1] = jnp.where(on_grid, value, -2.0)


def taps(foot_width):
    lane = lax.broadcasted_iota(jnp.int32, (BLOCK, TAPS), 1)
    tap_row = lane // REACH
    offset = (
        lane - tap_row * REACH - lax.broadcasted_iota(jnp.int32, (BLOCK, TAPS), 0) - HALO
    ).astype(jnp.float32)
    across = (tap_row[:1].astype(jnp.float32) - RAD) / (RAD + 1.0)
    norm = 3.0 / (2.0 * foot_width + 1.0)
    inside = jnp.abs(offset) <= foot_width
    along = offset * (1.0 / (foot_width + 1.0))
    pieces = []
    scales = [norm * jnp.maximum(0.0, 1.0 - 2.0 * jnp.abs(across - c)) for c in CENTERS]
    for lon_center in CENTERS:
        hat = jnp.maximum(0.0, 1.0 - 2.0 * jnp.abs(along - lon_center))
        hat = jnp.where(inside, hat, 0.0)
        pieces += [(hat * scale).astype(jnp.bfloat16) for scale in scales]
    return jnp.concatenate(pieces, axis=0)


def kernel(
    fields,
    cotangent,
    mixing,
    widths,
    features,
    gradient,
    cells,
    mixing_here,
    widths_here,
    straight,
    turned,
    wide,
    coeffs,
    basis,
    weights,
    load_sem,
    send_sem,
    recv_sem,
):
    rows, columns, channels = features.shape
    count = mixing.shape[0]
    inputs = (fields, cotangent)
    results = (features, gradient)
    here_lon, here_lat = lax.axis_index("lon"), lax.axis_index("lat")
    lons, lats = lax.axis_size("lon"), lax.axis_size("lat")
    east, west = lax.rem(here_lon + 1, lons), lax.rem(here_lon + lons - 1, lons)
    south, north = lax.rem(here_lat + 1, lats), lax.rem(here_lat + lats - 1, lats)

    barrier = pltpu.get_barrier_semaphore()
    for lat in (north, here_lat, south):
        for lon in (west, here_lon, east):
            if lat is here_lat and lon is here_lon:
                continue
            pl.semaphore_signal(
                barrier, inc=1, device_id=(lon, lat), device_id_type=pl.DeviceIdType.MESH
            )
    loads = []
    for side in range(2):
        load = pltpu.make_async_copy(
            inputs[side],
            cells.at[side, pl.ds(RAD, rows), pl.ds(HALO, columns)],
            load_sem.at[side],
        )
        load.start()
        loads.append(load)
    mix_load = pltpu.make_async_copy(mixing, mixing_here, load_sem.at[2])
    mix_load.start()
    width_load = pltpu.make_async_copy(widths, widths_here, load_sem.at[3])
    width_load.start()
    pl.semaphore_wait(barrier, 8)

    row_parts = (
        (north, 0, RAD, rows + RAD),
        (here_lat, 0, rows, RAD),
        (south, rows - RAD, RAD, 0),
    )
    column_parts = (
        (west, 0, HALO, columns + HALO),
        (here_lon, 0, columns, HALO),
        (east, columns - HALO, HALO, 0),
    )
    copies = {}
    for side in range(2):
        for place in ((0, 1), (2, 1), (1, 0), (1, 2), (0, 0), (0, 2), (2, 0), (2, 2)):
            lat, row_from, row_count, row_to = row_parts[place[0]]
            lon, column_from, column_count, column_to = column_parts[place[1]]
            slot = place[0] * 3 + place[1]
            copies[side, place] = pltpu.make_async_remote_copy(
                src_ref=inputs[side].at[pl.ds(row_from, row_count), pl.ds(column_from, column_count)],
                dst_ref=cells.at[side, pl.ds(row_to, row_count), pl.ds(column_to, column_count)],
                send_sem=send_sem.at[side, slot],
                recv_sem=recv_sem.at[side, slot],
                device_id=(lon, lat),
                device_id_type=pl.DeviceIdType.MESH,
            )
            copies[side, place].start()

    width_load.wait()
    widths_by_tap(widths_here, straight, turned, wide)
    mix_load.wait()
    for k in range(count):
        weights[0, k * channels : (k + 1) * channels, :] = mixing_here[k]
        weights[1, k * channels : (k + 1) * channels, :] = (
            mixing_here[count - 1 - k].astype(jnp.float32).T.astype(jnp.bfloat16)
        )

    def convolve(side, rows_here, parts, fresh):
        start, number, stride = rows_here

        def one_row(turn, carry):
            row = start + turn * stride
            if fresh:
                band = taps(wide[side, pl.ds(row, 1), :])
                coeffs[side, row] = band
            else:
                band = coeffs[side, row]
            data = jnp.concatenate(
                [
                    jnp.concatenate(
                        [
                            cells[side, row + r, BLOCK * b : BLOCK * b + REACH, :]
                            for r in range(SPAN)
                        ]
                        + [
                            cells[
                                side, row, BLOCK * b : BLOCK * b + TAPS - SPAN * REACH, :
                            ]
                        ],
                        axis=0,
                    )
                    for b in parts
                ],
                axis=1,
            )
            out = jnp.dot(band, data, preferred_element_type=jnp.float32).astype(jnp.bfloat16)
            for n in range(len(parts)):
                spot = (row * len(parts) + n) * BLOCK
                for k in range(count):
                    basis[side, pl.ds(spot, BLOCK), k * channels : (k + 1) * channels] = out[
                        k * BLOCK : (k + 1) * BLOCK, n * channels : (n + 1) * channels
                    ]
            return carry

        lax.fori_loop(0, number, one_row, 0, unroll=True)

    def mix(side, parts):
        size = rows * len(parts) * BLOCK
        mixed = jnp.dot(basis[side, :size, :], weights[side], preferred_element_type=jnp.float32)
        mixed = mixed.astype(jnp.bfloat16).reshape(rows, len(parts), BLOCK, channels)
        for n, b in enumerate(parts):
            results[side][:, BLOCK * b : BLOCK * (b + 1), :] = mixed[:, n]

    middle, rim = (1,), (0, 2)
    for side in range(2):
        loads[side].wait()
        convolve(side, (RAD, rows - 2 * RAD, 1), middle, True)
    for side in range(2):
        for place in ((0, 1), (2, 1)):
            copies[side, place].wait_recv()
    for side in range(2):
        convolve(side, (0, RAD, 1), middle, True)
        convolve(side, (rows - RAD, RAD, 1), middle, True)
    for side in range(2):
        mix(side, middle)
    for side in range(2):
        for place in ((1, 0), (1, 2), (0, 0), (0, 2), (2, 0), (2, 2)):
            copies[side, place].wait_recv()
        convolve(side, (0, rows, 1), rim, False)
        mix(side, rim)
    for copy in copies.values():
        copy.wait_send()


def body(fields, cotangent, mixing, widths):
    rows, columns, channels = fields.shape
    count = mixing.shape[0]
    shape = pltpu.VMEM(fields.shape, jnp.bfloat16)
    operands = [
        pltpu.with_memory_space_constraint(a, pltpu.HBM)
        for a in (fields, cotangent, mixing, widths.T)
    ]
    vmem = pl.BlockSpec(memory_space=pltpu.VMEM)
    hbm = pl.BlockSpec(memory_space=pltpu.HBM)
    return pl.pallas_call(
        kernel,
        out_shape=(shape, shape),
        in_specs=[hbm, hbm, hbm, hbm],
        out_specs=(vmem, vmem),
        scratch_shapes=[
            pltpu.VMEM((2, rows + 2 * RAD, columns + 2 * HALO, channels), jnp.bfloat16),
            pltpu.VMEM(mixing.shape, jnp.bfloat16),
            pltpu.VMEM((SPAN, widths.shape[0]), jnp.int32),
            pltpu.VMEM((widths.shape[0] + 16, TAPS), jnp.float32),
            pltpu.VMEM((widths.shape[0] + 16, TAPS), jnp.float32),
            pltpu.VMEM((2, rows, TAPS), jnp.float32),
            pltpu.VMEM((2, rows, count * BLOCK, TAPS), jnp.bfloat16),
            pltpu.VMEM((2, rows * 2 * BLOCK, count * channels), jnp.bfloat16),
            pltpu.VMEM((2, count * channels, channels), jnp.bfloat16),
            pltpu.SemaphoreType.DMA((4,)),
            pltpu.SemaphoreType.DMA((2, 9)),
            pltpu.SemaphoreType.DMA((2, 9)),
        ],
        compiler_params=pltpu.CompilerParams(
            collective_id=0, has_side_effects=True, vmem_limit_bytes=40 * 1024 * 1024
        ),
    )(*operands)


def solution(mesh):
    in_specs = (P("lat", "lon", None), P("lat", "lon", None), P(), P())
    out_specs = (P("lat", "lon", None), P("lat", "lon", None))
    return jax.shard_map(body, mesh=mesh, in_specs=in_specs, out_specs=out_specs, check_vma=False)
```

```python
import functools

import jax
import jax.numpy as jnp
from jax import lax
from jax.experimental import pallas as pl
from jax.experimental.pallas import tpu as pltpu
from jax.sharding import PartitionSpec as P

RAD = 2
HALO = 16
SPAN = 2 * RAD + 1
BLOCK = 16
REACH = BLOCK + 2 * HALO
TAPS = 256
CENTERS = (-0.5, 0.0, 0.5)


def widths_by_tap(widths, straight, turned, wide):
    rows = wide.shape[1]
    total = widths.shape[1]
    first = pl.multiple_of(lax.axis_index("lat") * rows, 8)
    source = lax.broadcasted_iota(jnp.int32, (SPAN, TAPS), 0)
    tap_row = lax.broadcasted_iota(jnp.int32, (SPAN, TAPS), 1) // REACH
    values = widths[...].astype(jnp.float32).astype(jnp.bfloat16)
    for pick, table in ((source == tap_row, straight), (source == SPAN - 1 - tap_row, turned)):
        table[:8] = jnp.zeros((8, TAPS), jnp.float32)
        table[total + 8 :] = jnp.zeros((8, TAPS), jnp.float32)
        table[8 : total + 8] = lax.dot_general(
            values,
            pick.astype(jnp.bfloat16),
            (((0,), (0,)), ((), ())),
            preferred_element_type=jnp.float32,
        )
    tap_row = lax.broadcasted_iota(jnp.int32, (rows, TAPS), 1) // REACH
    read = first + lax.broadcasted_iota(jnp.int32, (rows, TAPS), 0) + tap_row - RAD
    on_grid = (read >= 0) & (read < total)
    wide[0] = jnp.where(on_grid, straight[pl.ds(first + 8, rows), :], -2.0)
    near = turned[pl.ds(first, rows + 16), :]
    value = near[8 - RAD : 8 - RAD + rows]
    for r in range(1, SPAN):
        value = jnp.where(tap_row == r, near[8 - RAD + r : 8 - RAD + r + rows], value)
    wide[1] = jnp.where(on_grid, value, -2.0)


def taps(foot_width):
    lane = lax.broadcasted_iota(jnp.int32, (BLOCK, TAPS), 1)
    tap_row = lane // REACH
    offset = (
        lane - tap_row * REACH - lax.broadcasted_iota(jnp.int32, (BLOCK, TAPS), 0) - HALO
    ).astype(jnp.float32)
    across = (tap_row[:1].astype(jnp.float32) - RAD) / (RAD + 1.0)
    norm = 3.0 / (2.0 * foot_width + 1.0)
    inside = jnp.abs(offset) <= foot_width
    along = offset * (1.0 / (foot_width + 1.0))
    pieces = []
    scales = [norm * jnp.maximum(0.0, 1.0 - 2.0 * jnp.abs(across - c)) for c in CENTERS]
    for lon_center in CENTERS:
        hat = jnp.maximum(0.0, 1.0 - 2.0 * jnp.abs(along - lon_center))
        hat = jnp.where(inside, hat, 0.0)
        pieces += [(hat * scale).astype(jnp.bfloat16) for scale in scales]
    return jnp.concatenate(pieces, axis=0)


def kernel(
    fields,
    cotangent,
    mixing,
    widths,
    features,
    gradient,
    cells,
    mixing_here,
    widths_here,
    straight,
    turned,
    wide,
    coeffs,
    basis,
    edge_basis,
    weights,
    load_sem,
    send_sem,
    recv_sem,
    lon_in,
    lat_in,
):
    rows, columns, channels = features.shape
    count = mixing.shape[0]
    inputs = (fields, cotangent)
    results = (features, gradient)
    here_lon, here_lat = lax.axis_index("lon"), lax.axis_index("lat")
    lons, lats = lax.axis_size("lon"), lax.axis_size("lat")
    east, west = lax.rem(here_lon + 1, lons), lax.rem(here_lon + lons - 1, lons)
    south, north = lax.rem(here_lat + 1, lats), lax.rem(here_lat + lats - 1, lats)
    odd = lax.rem(here_lon, 2)
    lead = here_lon - odd
    barrier = pltpu.get_barrier_semaphore()

    def tell(sem, lon, lat):
        pl.semaphore_signal(sem, inc=1, device_id=(lon, lat), device_id_type=pl.DeviceIdType.MESH)

    @pl.when(odd == 0)
    def _():
        tell(barrier, lax.rem(here_lon + lons - 2, lons), here_lat)

    @pl.when(odd == 1)
    def _():
        tell(barrier, lead, here_lat)
        tell(barrier, east, here_lat)

    beside = lax.rem(here_lon + lons - 1 + 3 * odd, lons)
    for lat in (north, south):
        tell(barrier, lead + 1, lat)
        tell(barrier, beside, lat)

    loads = []
    for side in range(2):
        loads.append(
            pltpu.make_async_copy(
                inputs[side],
                cells.at[side, pl.ds(RAD, rows), pl.ds(HALO, columns)],
                load_sem.at[side],
            )
        )
    mix_load = pltpu.make_async_copy(mixing, mixing_here, load_sem.at[2])
    width_load = pltpu.make_async_copy(widths, widths_here, load_sem.at[3])
    for load in (*loads, width_load, mix_load):
        load.start()

    def remote(source, target, sems, lon, lat):
        return pltpu.make_async_remote_copy(
            src_ref=source,
            dst_ref=target,
            send_sem=sems[0].at[sems[1]],
            recv_sem=sems[2].at[sems[1]],
            device_id=(lon, lat),
            device_id_type=pl.DeviceIdType.MESH,
        )

    near_copies, far_copies, lat_copies = [], [], []
    last = columns + HALO
    mate = here_lon + 1 - 2 * odd
    away = lax.rem(here_lon + lons - 1 + 2 * odd, lons)
    low, high = pl.multiple_of(odd * last, HALO), pl.multiple_of((1 - odd) * last, HALO)
    near_take = pl.multiple_of((1 - odd) * (columns - HALO), HALO)
    far_take = pl.multiple_of(odd * (columns - HALO), HALO)
    for side in range(2):
        for slot, (copies, lon, take, give) in enumerate(
            ((near_copies, mate, near_take, low), (far_copies, away, far_take, high))
        ):
            copies.append(
                remote(
                    inputs[side].at[:, pl.ds(take, HALO)],
                    cells.at[side, pl.ds(RAD, rows), pl.ds(give, HALO)],
                    (send_sem, 2 * side + slot, recv_sem),
                    lon,
                    here_lat,
                )
            )
    for way, (lat, take, give) in enumerate(((north, RAD, rows + RAD), (south, rows, 0))):
        lat_copies.append(
            remote(
                cells.at[:, pl.ds(take, RAD), pl.ds(HALO, columns)],
                cells.at[:, pl.ds(give, RAD), pl.ds(HALO, columns)],
                (send_sem, 4 + way, recv_sem),
                here_lon,
                lat,
            )
        )
    corners = (
        (north, RAD, rows + RAD, west, HALO, last),
        (north, RAD, rows + RAD, east, columns, 0),
        (south, rows, 0, west, HALO, last),
        (south, rows, 0, east, columns, 0),
    )
    for slot, (lat, row_take, row_give, lon, take, give) in enumerate(corners):
        lat_copies.append(
            remote(
                cells.at[:, pl.ds(row_take, RAD), pl.ds(take, HALO)],
                cells.at[:, pl.ds(row_give, RAD), pl.ds(give, HALO)],
                (send_sem, 6 + slot, recv_sem),
                lon,
                lat,
            )
        )

    @pl.when(odd == 0)
    def _():
        pl.semaphore_wait(barrier, 3)
        tell(lon_in, lead + 1, here_lat)

    @pl.when(odd == 1)
    def _():
        pl.semaphore_wait(lon_in, 1)

    def send_lat():
        @pl.when(odd == 1)
        def _():
            pl.semaphore_wait(barrier, 8)
            tell(lat_in, lead, here_lat)

        @pl.when(odd == 0)
        def _():
            pl.semaphore_wait(lat_in, 1)

        for copy in lat_copies:
            copy.start()

    for copy in near_copies:
        copy.start()
    for load in loads:
        load.wait()

    @pl.when(lax.rem(here_lat, 2) == 1)
    def _():
        send_lat()

    for copy in far_copies:
        copy.start()

    width_load.wait()
    widths_by_tap(widths_here, straight, turned, wide)
    mix_load.wait()
    for k in range(count):
        weights[0, k * channels : (k + 1) * channels, :] = mixing_here[k]
        weights[1, k * channels : (k + 1) * channels, :] = (
            mixing_here[count - 1 - k].astype(jnp.float32).T.astype(jnp.bfloat16)
        )

    def convolve(side, row, spot, target, parts, fresh):
        if fresh:
            band = taps(wide[side, pl.ds(row, 1), :])
            coeffs[side, row] = band
        else:
            band = coeffs[side, row]
        data = jnp.concatenate(
            [
                jnp.concatenate(
                    [cells[side, row + r, pl.ds(b, REACH), :] for r in range(SPAN)]
                    + [cells[side, row, pl.ds(b, TAPS - SPAN * REACH), :]],
                    axis=0,
                )
                for b in parts
            ],
            axis=1,
        )
        out = jnp.dot(band, data, preferred_element_type=jnp.float32).astype(jnp.bfloat16)
        for n in range(len(parts)):
            for k in range(count):
                target[
                    side, pl.ds(spot + n * BLOCK, BLOCK), k * channels : (k + 1) * channels
                ] = out[k * BLOCK : (k + 1) * BLOCK, n * channels : (n + 1) * channels]

    def convolve_inner(side, parts, fresh):
        def one_row(row, carry):
            spot = (row - RAD) * len(parts) * BLOCK
            convolve(side, row, spot, basis, parts, fresh)
            return carry

        lax.fori_loop(RAD, rows - RAD, one_row, 0, unroll=True)

    def mix_inner(side, parts):
        size = (rows - 2 * RAD) * len(parts) * BLOCK
        mixed = jnp.dot(basis[side, :size, :], weights[side], preferred_element_type=jnp.float32)
        mixed = mixed.astype(jnp.bfloat16).reshape(-1, len(parts), BLOCK, channels)
        for n, b in enumerate(parts):
            results[side][RAD : rows - RAD, pl.ds(b, BLOCK), :] = mixed[:, n]

    near = pl.multiple_of((1 - odd) * (columns - BLOCK), BLOCK)
    far = pl.multiple_of(odd * (columns - BLOCK), BLOCK)
    for side in range(2):
        near_copies[side].wait_recv()
        convolve_inner(side, (BLOCK, near), True)
    for side in range(2):
        mix_inner(side, (BLOCK, near))

    @pl.when(lax.rem(here_lat, 2) == 0)
    def _():
        send_lat()

    for side in range(2):
        far_copies[side].wait_recv()
        convolve_inner(side, (far,), False)
        mix_inner(side, (far,))

    for copy in lat_copies:
        copy.wait_recv()
    outer = (*range(RAD), *range(rows - RAD, rows))
    whole = (0, BLOCK, 2 * BLOCK)
    for side in range(2):
        for e, row in enumerate(outer):
            convolve(side, row, e * columns, edge_basis, whole, True)
    for side in range(2):
        mixed = jnp.dot(edge_basis[side], weights[side], preferred_element_type=jnp.float32)
        mixed = mixed.astype(jnp.bfloat16).reshape(len(outer), columns, channels)
        for e, row in enumerate(outer):
            results[side][row] = mixed[e]
    for copy in (*near_copies, *far_copies, *lat_copies):
        copy.wait_send()


def body(fields, cotangent, mixing, widths):
    rows, columns, channels = fields.shape
    count = mixing.shape[0]
    shape = pltpu.VMEM(fields.shape, jnp.bfloat16)
    operands = [
        pltpu.with_memory_space_constraint(a, pltpu.HBM)
        for a in (fields, cotangent, mixing, widths.T)
    ]
    vmem = pl.BlockSpec(memory_space=pltpu.VMEM)
    hbm = pl.BlockSpec(memory_space=pltpu.HBM)
    return pl.pallas_call(
        kernel,
        out_shape=(shape, shape),
        in_specs=[hbm, hbm, hbm, hbm],
        out_specs=(vmem, vmem),
        scratch_shapes=[
            pltpu.VMEM((2, rows + 2 * RAD, columns + 2 * HALO, channels), jnp.bfloat16),
            pltpu.VMEM(mixing.shape, jnp.bfloat16),
            pltpu.VMEM((SPAN, widths.shape[0]), jnp.int32),
            pltpu.VMEM((widths.shape[0] + 16, TAPS), jnp.float32),
            pltpu.VMEM((widths.shape[0] + 16, TAPS), jnp.float32),
            pltpu.VMEM((2, rows, TAPS), jnp.float32),
            pltpu.VMEM((2, rows, count * BLOCK, TAPS), jnp.bfloat16),
            pltpu.VMEM((2, rows * 2 * BLOCK, count * channels), jnp.bfloat16),
            pltpu.VMEM((2, 2 * RAD * columns, count * channels), jnp.bfloat16),
            pltpu.VMEM((2, count * channels, channels), jnp.bfloat16),
            pltpu.SemaphoreType.DMA((4,)),
            pltpu.SemaphoreType.DMA((10,)),
            pltpu.SemaphoreType.DMA((10,)),
            pltpu.SemaphoreType.REGULAR,
            pltpu.SemaphoreType.REGULAR,
        ],
        compiler_params=pltpu.CompilerParams(
            collective_id=0, has_side_effects=True, vmem_limit_bytes=40 * 1024 * 1024
        ),
    )(*operands)


def solution(mesh):
    in_specs = (P("lat", "lon", None), P("lat", "lon", None), P(), P())
    out_specs = (P("lat", "lon", None), P("lat", "lon", None))
    return jax.shard_map(body, mesh=mesh, in_specs=in_specs, out_specs=out_specs, check_vma=False)
```

```python
import functools

import jax
import jax.numpy as jnp
from jax import lax
from jax.experimental import pallas as pl
from jax.experimental.pallas import tpu as pltpu
from jax.sharding import PartitionSpec as P

RAD = 2
HALO = 16
SPAN = 2 * RAD + 1
BLOCK = 16
REACH = BLOCK + 2 * HALO
TAPS = 256
RUN = 8
CENTERS = (-0.5, 0.0, 0.5)


def widths_by_tap(widths, straight, turned, wide):
    rows = wide.shape[1]
    total = widths.shape[1]
    first = pl.multiple_of(lax.axis_index("lat") * rows, 8)
    source = lax.broadcasted_iota(jnp.int32, (SPAN, TAPS), 0)
    tap_row = lax.broadcasted_iota(jnp.int32, (SPAN, TAPS), 1) // REACH
    values = widths[...].astype(jnp.float32).astype(jnp.bfloat16)
    for pick, table in ((source == tap_row, straight), (source == SPAN - 1 - tap_row, turned)):
        table[:8] = jnp.zeros((8, TAPS), jnp.float32)
        table[total + 8 :] = jnp.zeros((8, TAPS), jnp.float32)
        table[8 : total + 8] = lax.dot_general(
            values,
            pick.astype(jnp.bfloat16),
            (((0,), (0,)), ((), ())),
            preferred_element_type=jnp.float32,
        )
    tap_row = lax.broadcasted_iota(jnp.int32, (rows, TAPS), 1) // REACH
    read = first + lax.broadcasted_iota(jnp.int32, (rows, TAPS), 0) + tap_row - RAD
    on_grid = (read >= 0) & (read < total)
    wide[0] = jnp.where(on_grid, straight[pl.ds(first + 8, rows), :], -2.0)
    near = turned[pl.ds(first, rows + 16), :]
    value = near[8 - RAD : 8 - RAD + rows]
    for r in range(1, SPAN):
        value = jnp.where(tap_row == r, near[8 - RAD + r : 8 - RAD + r + rows], value)
    wide[1] = jnp.where(on_grid, value, -2.0)


def taps(foot_width):
    lane = lax.broadcasted_iota(jnp.int32, (BLOCK, TAPS), 1)
    tap_row = lane // REACH
    offset = (
        lane - tap_row * REACH - lax.broadcasted_iota(jnp.int32, (BLOCK, TAPS), 0) - HALO
    ).astype(jnp.float32)
    across = (tap_row[:1].astype(jnp.float32) - RAD) / (RAD + 1.0)
    norm = 3.0 / (2.0 * foot_width + 1.0)
    inside = jnp.abs(offset) <= foot_width
    along = offset * (1.0 / (foot_width + 1.0))
    pieces = []
    scales = [norm * jnp.maximum(0.0, 1.0 - 2.0 * jnp.abs(across - c)) for c in CENTERS]
    for lon_center in CENTERS:
        hat = jnp.maximum(0.0, 1.0 - 2.0 * jnp.abs(along - lon_center))
        hat = jnp.where(inside, hat, 0.0)
        pieces += [(hat * scale).astype(jnp.bfloat16) for scale in scales]
    return jnp.concatenate(pieces, axis=0)


def kernel(
    fields,
    cotangent,
    mixing,
    widths,
    features,
    gradient,
    cells,
    mixing_here,
    widths_here,
    straight,
    turned,
    wide,
    coeffs,
    basis,
    edge_basis,
    weights,
    load_sem,
    send_sem,
    recv_sem,
    lon_in,
    lat_in,
):
    rows, columns, channels = features.shape
    count = mixing.shape[0]
    inputs = (fields, cotangent)
    results = (features, gradient)
    here_lon, here_lat = lax.axis_index("lon"), lax.axis_index("lat")
    lons, lats = lax.axis_size("lon"), lax.axis_size("lat")
    east, west = lax.rem(here_lon + 1, lons), lax.rem(here_lon + lons - 1, lons)
    south, north = lax.rem(here_lat + 1, lats), lax.rem(here_lat + lats - 1, lats)
    odd = lax.rem(here_lon, 2)
    lead = here_lon - odd
    barrier = pltpu.get_barrier_semaphore()

    def tell(sem, lon, lat):
        pl.semaphore_signal(sem, inc=1, device_id=(lon, lat), device_id_type=pl.DeviceIdType.MESH)

    @pl.when(odd == 0)
    def _():
        tell(barrier, lax.rem(here_lon + lons - 2, lons), here_lat)

    @pl.when(odd == 1)
    def _():
        tell(barrier, lead, here_lat)
        tell(barrier, east, here_lat)

    beside = lax.rem(here_lon + lons - 1 + 3 * odd, lons)
    for lat in (north, south):
        tell(barrier, lead + 1, lat)
        tell(barrier, beside, lat)

    loads = []
    for side in range(2):
        loads.append(
            pltpu.make_async_copy(
                inputs[side],
                cells.at[side, pl.ds(RAD, rows), pl.ds(HALO, columns)],
                load_sem.at[side],
            )
        )
    mix_load = pltpu.make_async_copy(mixing, mixing_here, load_sem.at[2])
    width_load = pltpu.make_async_copy(widths, widths_here, load_sem.at[3])
    for load in (*loads, width_load, mix_load):
        load.start()

    def remote(source, target, sems, lon, lat):
        return pltpu.make_async_remote_copy(
            src_ref=source,
            dst_ref=target,
            send_sem=sems[0].at[sems[1]],
            recv_sem=sems[2].at[sems[1]],
            device_id=(lon, lat),
            device_id_type=pl.DeviceIdType.MESH,
        )

    near_copies, far_copies, lat_copies = [], [], []
    last = columns + HALO
    mate = here_lon + 1 - 2 * odd
    away = lax.rem(here_lon + lons - 1 + 2 * odd, lons)
    low, high = pl.multiple_of(odd * last, HALO), pl.multiple_of((1 - odd) * last, HALO)
    near_take = pl.multiple_of((1 - odd) * (columns - HALO), HALO)
    far_take = pl.multiple_of(odd * (columns - HALO), HALO)
    for side in range(2):
        for slot, (copies, lon, take, give) in enumerate(
            ((near_copies, mate, near_take, low), (far_copies, away, far_take, high))
        ):
            copies.append(
                remote(
                    inputs[side].at[:, pl.ds(take, HALO)],
                    cells.at[side, pl.ds(RAD, rows), pl.ds(give, HALO)],
                    (send_sem, 2 * side + slot, recv_sem),
                    lon,
                    here_lat,
                )
            )
    for way, (lat, take, give) in enumerate(((north, RAD, rows + RAD), (south, rows, 0))):
        lat_copies.append(
            remote(
                cells.at[:, pl.ds(take, RAD), pl.ds(HALO, columns)],
                cells.at[:, pl.ds(give, RAD), pl.ds(HALO, columns)],
                (send_sem, 4 + way, recv_sem),
                here_lon,
                lat,
            )
        )
    corners = (
        (north, RAD, rows + RAD, west, HALO, last),
        (north, RAD, rows + RAD, east, columns, 0),
        (south, rows, 0, west, HALO, last),
        (south, rows, 0, east, columns, 0),
    )
    for slot, (lat, row_take, row_give, lon, take, give) in enumerate(corners):
        lat_copies.append(
            remote(
                cells.at[:, pl.ds(row_take, RAD), pl.ds(take, HALO)],
                cells.at[:, pl.ds(row_give, RAD), pl.ds(give, HALO)],
                (send_sem, 6 + slot, recv_sem),
                lon,
                lat,
            )
        )

    @pl.when(odd == 0)
    def _():
        pl.semaphore_wait(barrier, 3)
        tell(lon_in, lead + 1, here_lat)

    @pl.when(odd == 1)
    def _():
        pl.semaphore_wait(lon_in, 1)

    def send_lat():
        @pl.when(odd == 1)
        def _():
            pl.semaphore_wait(barrier, 8)
            tell(lat_in, lead, here_lat)

        @pl.when(odd == 0)
        def _():
            pl.semaphore_wait(lat_in, 1)

        for copy in lat_copies:
            copy.start()

    for copy in near_copies:
        copy.start()
    for load in loads:
        load.wait()

    @pl.when(lax.rem(here_lat, 2) == 1)
    def _():
        send_lat()

    for copy in far_copies:
        copy.start()

    width_load.wait()
    widths_by_tap(widths_here, straight, turned, wide)
    mix_load.wait()
    for k in range(count):
        weights[0, k * channels : (k + 1) * channels, :] = mixing_here[k]
        weights[1, k * channels : (k + 1) * channels, :] = (
            mixing_here[count - 1 - k].astype(jnp.float32).T.astype(jnp.bfloat16)
        )

    def convolve(side, row, spot, target, parts, fresh):
        if fresh:
            band = taps(wide[side, pl.ds(row, 1), :])
            coeffs[side, row] = band
        else:
            band = coeffs[side, row]
        data = jnp.concatenate(
            [
                jnp.concatenate(
                    [cells[side, row + r, pl.ds(b, REACH), :] for r in range(SPAN)]
                    + [cells[side, row, pl.ds(b, TAPS - SPAN * REACH), :]],
                    axis=0,
                )
                for b in parts
            ],
            axis=1,
        )
        out = jnp.dot(band, data, preferred_element_type=jnp.float32).astype(jnp.bfloat16)
        for n in range(len(parts)):
            for k in range(count):
                target[
                    side, pl.ds(spot + n * BLOCK, BLOCK), k * channels : (k + 1) * channels
                ] = out[k * BLOCK : (k + 1) * BLOCK, n * channels : (n + 1) * channels]

    def convolve_inner(side, parts, fresh):
        def one_row(row, carry):
            spot = (row - RAD) * len(parts) * BLOCK
            convolve(side, row, spot, basis, parts, fresh)
            return carry

        lax.fori_loop(RAD, rows - RAD, one_row, 0, unroll=True)

    def mix_inner(side, parts):
        size = (rows - 2 * RAD) * len(parts) * BLOCK
        mixed = jnp.dot(basis[side, :size, :], weights[side], preferred_element_type=jnp.float32)
        mixed = mixed.astype(jnp.bfloat16).reshape(-1, len(parts), BLOCK, channels)
        for n, b in enumerate(parts):
            results[side][RAD : rows - RAD, pl.ds(b, BLOCK), :] = mixed[:, n]

    near = pl.multiple_of((1 - odd) * (columns - BLOCK), BLOCK)
    far = pl.multiple_of(odd * (columns - BLOCK), BLOCK)
    for side in range(2):
        near_copies[side].wait_recv()
        convolve_inner(side, (BLOCK, near), True)
    for side in range(2):
        mix_inner(side, (BLOCK, near))

    @pl.when(lax.rem(here_lat, 2) == 0)
    def _():
        send_lat()

    def far_rows(side, first, number):
        def one_row(row, carry):
            convolve(side, row, (row - first) * BLOCK, basis, (far,), False)
            return carry

        lax.fori_loop(first, first + number, one_row, 0, unroll=True)
        mixed = jnp.dot(
            basis[side, : number * BLOCK, :], weights[side], preferred_element_type=jnp.float32
        )
        results[side][first : first + number, pl.ds(far, BLOCK), :] = (
            mixed.astype(jnp.bfloat16).reshape(number, BLOCK, channels)
        )

    def edge_rows(parts):
        outer = (*range(RAD), *range(rows - RAD, rows))
        for side in range(2):
            for e, row in enumerate(outer):
                convolve(side, row, e * len(parts) * BLOCK, edge_basis, parts, True)
        size = len(outer) * len(parts) * BLOCK
        for side in range(2):
            mixed = jnp.dot(
                edge_basis[side, :size, :], weights[side], preferred_element_type=jnp.float32
            )
            mixed = mixed.astype(jnp.bfloat16).reshape(len(outer), len(parts), BLOCK, channels)
            for e, row in enumerate(outer):
                for n, b in enumerate(parts):
                    results[side][row, pl.ds(b, BLOCK), :] = mixed[e, n]

    place = lax.rem(here_lon + 1, RUN)
    far_last = (lax.rem(here_lat, 2) == 1) & (place <= 1)

    @pl.when(far_last)
    def _():
        for copy in lat_copies:
            copy.wait_recv()
        edge_rows((BLOCK, near))
        for side in range(2):
            far_copies[side].wait_recv()
            far_rows(side, 0, rows)

    @pl.when(jnp.logical_not(far_last))
    def _():
        for side in range(2):
            far_copies[side].wait_recv()
            far_rows(side, RAD, rows - 2 * RAD)
        for copy in lat_copies:
            copy.wait_recv()
        edge_rows((0, BLOCK, 2 * BLOCK))

    for copy in (*near_copies, *far_copies, *lat_copies):
        copy.wait_send()


def deliver(features, gradient, features_out, gradient_out, sem):
    copies = [
        pltpu.make_async_copy(features, features_out, sem.at[0]),
        pltpu.make_async_copy(gradient, gradient_out, sem.at[1]),
    ]
    for copy in copies:
        copy.start()
    for copy in copies:
        copy.wait()


def body(fields, cotangent, mixing, widths):
    rows, columns, channels = fields.shape
    count = mixing.shape[0]
    shape = pltpu.VMEM(fields.shape, jnp.bfloat16)
    operands = [
        pltpu.with_memory_space_constraint(a, pltpu.HBM)
        for a in (fields, cotangent, mixing, widths.T)
    ]
    vmem = pl.BlockSpec(memory_space=pltpu.VMEM)
    hbm = pl.BlockSpec(memory_space=pltpu.HBM)
    results = pl.pallas_call(
        kernel,
        out_shape=(shape, shape),
        in_specs=[hbm, hbm, hbm, hbm],
        out_specs=(vmem, vmem),
        scratch_shapes=[
            pltpu.VMEM((2, rows + 2 * RAD, columns + 2 * HALO, channels), jnp.bfloat16),
            pltpu.VMEM(mixing.shape, jnp.bfloat16),
            pltpu.VMEM((SPAN, widths.shape[0]), jnp.int32),
            pltpu.VMEM((widths.shape[0] + 16, TAPS), jnp.float32),
            pltpu.VMEM((widths.shape[0] + 16, TAPS), jnp.float32),
            pltpu.VMEM((2, rows, TAPS), jnp.float32),
            pltpu.VMEM((2, rows, count * BLOCK, TAPS), jnp.bfloat16),
            pltpu.VMEM((2, rows * 2 * BLOCK, count * channels), jnp.bfloat16),
            pltpu.VMEM((2, 2 * RAD * columns, count * channels), jnp.bfloat16),
            pltpu.VMEM((2, count * channels, channels), jnp.bfloat16),
            pltpu.SemaphoreType.DMA((4,)),
            pltpu.SemaphoreType.DMA((10,)),
            pltpu.SemaphoreType.DMA((10,)),
            pltpu.SemaphoreType.REGULAR,
            pltpu.SemaphoreType.REGULAR,
        ],
        compiler_params=pltpu.CompilerParams(
            collective_id=0, has_side_effects=True, vmem_limit_bytes=40 * 1024 * 1024
        ),
    )(*operands)
    results = [pltpu.with_memory_space_constraint(a, pltpu.VMEM) for a in results]
    anywhere = pl.BlockSpec(memory_space=pl.ANY)
    final = jax.ShapeDtypeStruct(fields.shape, jnp.bfloat16)
    return pl.pallas_call(
        deliver,
        out_shape=(final, final),
        in_specs=[vmem, vmem],
        out_specs=(anywhere, anywhere),
        scratch_shapes=[pltpu.SemaphoreType.DMA((2,))],
    )(*results)


def solution(mesh):
    in_specs = (P("lat", "lon", None), P("lat", "lon", None), P(), P())
    out_specs = (P("lat", "lon", None), P("lat", "lon", None))
    return jax.shard_map(body, mesh=mesh, in_specs=in_specs, out_specs=out_specs, check_vma=False)
```

```python
import functools

import jax
import jax.numpy as jnp
from jax import lax
from jax.experimental import pallas as pl
from jax.experimental.pallas import tpu as pltpu
from jax.sharding import PartitionSpec as P

RAD = 2
HALO = 16
SPAN = 2 * RAD + 1
BLOCK = 16
REACH = BLOCK + 2 * HALO
TAPS = 256
RUN = 8
CENTERS = (-0.5, 0.0, 0.5)


def widths_by_tap(widths, straight, turned, wide):
    rows = wide.shape[1]
    total = widths.shape[1]
    first = pl.multiple_of(lax.axis_index("lat") * rows, 8)
    source = lax.broadcasted_iota(jnp.int32, (SPAN, TAPS), 0)
    tap_row = lax.broadcasted_iota(jnp.int32, (SPAN, TAPS), 1) // REACH
    values = widths[...].astype(jnp.float32).astype(jnp.bfloat16)
    for pick, table in ((source == tap_row, straight), (source == SPAN - 1 - tap_row, turned)):
        table[:8] = jnp.zeros((8, TAPS), jnp.float32)
        table[total + 8 :] = jnp.zeros((8, TAPS), jnp.float32)
        table[8 : total + 8] = lax.dot_general(
            values,
            pick.astype(jnp.bfloat16),
            (((0,), (0,)), ((), ())),
            preferred_element_type=jnp.float32,
        )
    tap_row = lax.broadcasted_iota(jnp.int32, (rows, TAPS), 1) // REACH
    read = first + lax.broadcasted_iota(jnp.int32, (rows, TAPS), 0) + tap_row - RAD
    on_grid = (read >= 0) & (read < total)
    wide[0] = jnp.where(on_grid, straight[pl.ds(first + 8, rows), :], -2.0)
    near = turned[pl.ds(first, rows + 16), :]
    value = near[8 - RAD : 8 - RAD + rows]
    for r in range(1, SPAN):
        value = jnp.where(tap_row == r, near[8 - RAD + r : 8 - RAD + r + rows], value)
    wide[1] = jnp.where(on_grid, value, -2.0)


def taps(foot_width):
    lane = lax.broadcasted_iota(jnp.int32, (BLOCK, TAPS), 1)
    tap_row = lane // REACH
    offset = (
        lane - tap_row * REACH - lax.broadcasted_iota(jnp.int32, (BLOCK, TAPS), 0) - HALO
    ).astype(jnp.float32)
    across = (tap_row[:1].astype(jnp.float32) - RAD) / (RAD + 1.0)
    norm = 3.0 / (2.0 * foot_width + 1.0)
    inside = jnp.abs(offset) <= foot_width
    along = offset * (1.0 / (foot_width + 1.0))
    pieces = []
    scales = [norm * jnp.maximum(0.0, 1.0 - 2.0 * jnp.abs(across - c)) for c in CENTERS]
    for lon_center in CENTERS:
        hat = jnp.maximum(0.0, 1.0 - 2.0 * jnp.abs(along - lon_center))
        hat = jnp.where(inside, hat, 0.0)
        pieces += [(hat * scale).astype(jnp.bfloat16) for scale in scales]
    return jnp.concatenate(pieces, axis=0)


def kernel(
    fields,
    cotangent,
    mixing,
    widths,
    features,
    gradient,
    cells,
    mixing_here,
    widths_here,
    straight,
    turned,
    wide,
    coeffs,
    basis,
    edge_basis,
    weights,
    load_sem,
    send_sem,
    recv_sem,
    lon_in,
    lat_in,
):
    rows, columns, channels = features.shape
    count = mixing.shape[0]
    inputs = (fields, cotangent)
    results = (features, gradient)
    here_lon, here_lat = lax.axis_index("lon"), lax.axis_index("lat")
    lons, lats = lax.axis_size("lon"), lax.axis_size("lat")
    east, west = lax.rem(here_lon + 1, lons), lax.rem(here_lon + lons - 1, lons)
    south, north = lax.rem(here_lat + 1, lats), lax.rem(here_lat + lats - 1, lats)
    odd = lax.rem(here_lon, 2)
    lead = here_lon - odd
    barrier = pltpu.get_barrier_semaphore()

    def tell(sem, lon, lat):
        pl.semaphore_signal(sem, inc=1, device_id=(lon, lat), device_id_type=pl.DeviceIdType.MESH)

    @pl.when(odd == 0)
    def _():
        tell(barrier, lax.rem(here_lon + lons - 2, lons), here_lat)

    @pl.when(odd == 1)
    def _():
        tell(barrier, lead, here_lat)
        tell(barrier, east, here_lat)

    beside = lax.rem(here_lon + lons - 1 + 3 * odd, lons)
    for lat in (north, south):
        tell(barrier, lead + 1, lat)
        tell(barrier, beside, lat)

    loads = []
    for side in range(2):
        loads.append(
            pltpu.make_async_copy(
                inputs[side],
                cells.at[side, pl.ds(RAD, rows), pl.ds(HALO, columns)],
                load_sem.at[side],
            )
        )
    mix_load = pltpu.make_async_copy(mixing, mixing_here, load_sem.at[2])
    width_load = pltpu.make_async_copy(widths, widths_here, load_sem.at[3])
    for load in (*loads, width_load, mix_load):
        load.start()

    def remote(source, target, sems, lon, lat):
        return pltpu.make_async_remote_copy(
            src_ref=source,
            dst_ref=target,
            send_sem=sems[0].at[sems[1]],
            recv_sem=sems[2].at[sems[1]],
            device_id=(lon, lat),
            device_id_type=pl.DeviceIdType.MESH,
        )

    near_copies, far_copies, lat_copies = [], [], []
    last = columns + HALO
    mate = here_lon + 1 - 2 * odd
    away = lax.rem(here_lon + lons - 1 + 2 * odd, lons)
    low, high = pl.multiple_of(odd * last, HALO), pl.multiple_of((1 - odd) * last, HALO)
    near_take = pl.multiple_of((1 - odd) * (columns - HALO), HALO)
    far_take = pl.multiple_of(odd * (columns - HALO), HALO)
    for side in range(2):
        for slot, (copies, lon, take, give) in enumerate(
            ((near_copies, mate, near_take, low), (far_copies, away, far_take, high))
        ):
            copies.append(
                remote(
                    inputs[side].at[:, pl.ds(take, HALO)],
                    cells.at[side, pl.ds(RAD, rows), pl.ds(give, HALO)],
                    (send_sem, 2 * side + slot, recv_sem),
                    lon,
                    here_lat,
                )
            )
    for way, (lat, take, give) in enumerate(((north, RAD, rows + RAD), (south, rows, 0))):
        lat_copies.append(
            remote(
                cells.at[:, pl.ds(take, RAD), pl.ds(HALO, columns)],
                cells.at[:, pl.ds(give, RAD), pl.ds(HALO, columns)],
                (send_sem, 4 + way, recv_sem),
                here_lon,
                lat,
            )
        )
    corners = (
        (north, RAD, rows + RAD, west, HALO, last),
        (north, RAD, rows + RAD, east, columns, 0),
        (south, rows, 0, west, HALO, last),
        (south, rows, 0, east, columns, 0),
    )
    for slot, (lat, row_take, row_give, lon, take, give) in enumerate(corners):
        lat_copies.append(
            remote(
                cells.at[:, pl.ds(row_take, RAD), pl.ds(take, HALO)],
                cells.at[:, pl.ds(row_give, RAD), pl.ds(give, HALO)],
                (send_sem, 6 + slot, recv_sem),
                lon,
                lat,
            )
        )

    @pl.when(odd == 0)
    def _():
        pl.semaphore_wait(barrier, 3)
        tell(lon_in, lead + 1, here_lat)

    @pl.when(odd == 1)
    def _():
        pl.semaphore_wait(lon_in, 1)

    def send_lat():
        @pl.when(odd == 1)
        def _():
            pl.semaphore_wait(barrier, 8)
            tell(lat_in, lead, here_lat)

        @pl.when(odd == 0)
        def _():
            pl.semaphore_wait(lat_in, 1)

        for copy in lat_copies:
            copy.start()

    for copy in near_copies:
        copy.start()
    for load in loads:
        load.wait()

    @pl.when(lax.rem(here_lat, 2) == 1)
    def _():
        send_lat()

    for copy in far_copies:
        copy.start()

    width_load.wait()
    widths_by_tap(widths_here, straight, turned, wide)
    mix_load.wait()
    for k in range(count):
        weights[0, k * channels : (k + 1) * channels, :] = mixing_here[k]
        weights[1, k * channels : (k + 1) * channels, :] = (
            mixing_here[count - 1 - k].astype(jnp.float32).T.astype(jnp.bfloat16)
        )

    def convolve(side, row, spot, target, parts, fresh):
        if fresh:
            band = taps(wide[side, pl.ds(row, 1), :])
            coeffs[side, row] = band
        else:
            band = coeffs[side, row]
        data = jnp.concatenate(
            [
                jnp.concatenate(
                    [cells[side, row + r, pl.ds(b, REACH), :] for r in range(SPAN)]
                    + [cells[side, row, pl.ds(b, TAPS - SPAN * REACH), :]],
                    axis=0,
                )
                for b in parts
            ],
            axis=1,
        )
        out = jnp.dot(band, data, preferred_element_type=jnp.float32).astype(jnp.bfloat16)
        for n in range(len(parts)):
            for k in range(count):
                target[
                    side, pl.ds(spot + n * BLOCK, BLOCK), k * channels : (k + 1) * channels
                ] = out[k * BLOCK : (k + 1) * BLOCK, n * channels : (n + 1) * channels]

    def convolve_inner(side, parts, fresh):
        def one_row(row, carry):
            spot = (row - RAD) * len(parts) * BLOCK
            convolve(side, row, spot, basis, parts, fresh)
            return carry

        lax.fori_loop(RAD, rows - RAD, one_row, 0, unroll=True)

    def mix_inner(side, parts):
        size = (rows - 2 * RAD) * len(parts) * BLOCK
        mixed = jnp.dot(basis[side, :size, :], weights[side], preferred_element_type=jnp.float32)
        mixed = mixed.astype(jnp.bfloat16).reshape(-1, len(parts), BLOCK, channels)
        for n, b in enumerate(parts):
            results[side][RAD : rows - RAD, pl.ds(b, BLOCK), :] = mixed[:, n]

    near = pl.multiple_of((1 - odd) * (columns - BLOCK), BLOCK)
    far = pl.multiple_of(odd * (columns - BLOCK), BLOCK)
    for side in range(2):
        near_copies[side].wait_recv()
        convolve_inner(side, (BLOCK, near), True)
    for side in range(2):
        mix_inner(side, (BLOCK, near))

    for side in range(2):
        for row in (*range(RAD), *range(rows - RAD, rows)):
            coeffs[side, row] = taps(wide[side, pl.ds(row, 1), :])

    @pl.when(lax.rem(here_lat, 2) == 0)
    def _():
        send_lat()

    def far_rows(side, first, number):
        def one_row(row, carry):
            convolve(side, row, (row - first) * BLOCK, basis, (far,), False)
            return carry

        lax.fori_loop(first, first + number, one_row, 0, unroll=True)
        mixed = jnp.dot(
            basis[side, : number * BLOCK, :], weights[side], preferred_element_type=jnp.float32
        )
        results[side][first : first + number, pl.ds(far, BLOCK), :] = (
            mixed.astype(jnp.bfloat16).reshape(number, BLOCK, channels)
        )

    def edge_rows(parts):
        outer = (*range(RAD), *range(rows - RAD, rows))
        for side in range(2):
            for e, row in enumerate(outer):
                convolve(side, row, e * len(parts) * BLOCK, edge_basis, parts, False)
        size = len(outer) * len(parts) * BLOCK
        for side in range(2):
            mixed = jnp.dot(
                edge_basis[side, :size, :], weights[side], preferred_element_type=jnp.float32
            )
            mixed = mixed.astype(jnp.bfloat16).reshape(len(outer), len(parts), BLOCK, channels)
            for e, row in enumerate(outer):
                for n, b in enumerate(parts):
                    results[side][row, pl.ds(b, BLOCK), :] = mixed[e, n]

    place = lax.rem(here_lon + 1, RUN)
    far_last = (lax.rem(here_lat, 2) == 1) & (place <= 1)

    @pl.when(far_last)
    def _():
        for copy in lat_copies:
            copy.wait_recv()
        edge_rows((BLOCK, near))
        for side in range(2):
            far_copies[side].wait_recv()
            far_rows(side, 0, rows)

    @pl.when(jnp.logical_not(far_last))
    def _():
        for side in range(2):
            far_copies[side].wait_recv()
            far_rows(side, RAD, rows - 2 * RAD)
        for copy in lat_copies:
            copy.wait_recv()
        edge_rows((0, BLOCK, 2 * BLOCK))

    for copy in (*near_copies, *far_copies, *lat_copies):
        copy.wait_send()


def deliver(features, gradient, features_out, gradient_out, sem):
    copies = [
        pltpu.make_async_copy(features, features_out, sem.at[0]),
        pltpu.make_async_copy(gradient, gradient_out, sem.at[1]),
    ]
    for copy in copies:
        copy.start()
    for copy in copies:
        copy.wait()


def body(fields, cotangent, mixing, widths):
    rows, columns, channels = fields.shape
    count = mixing.shape[0]
    shape = pltpu.VMEM(fields.shape, jnp.bfloat16)
    operands = [
        pltpu.with_memory_space_constraint(a, pltpu.HBM)
        for a in (fields, cotangent, mixing, widths.T)
    ]
    vmem = pl.BlockSpec(memory_space=pltpu.VMEM)
    hbm = pl.BlockSpec(memory_space=pltpu.HBM)
    results = pl.pallas_call(
        kernel,
        out_shape=(shape, shape),
        in_specs=[hbm, hbm, hbm, hbm],
        out_specs=(vmem, vmem),
        scratch_shapes=[
            pltpu.VMEM((2, rows + 2 * RAD, columns + 2 * HALO, channels), jnp.bfloat16),
            pltpu.VMEM(mixing.shape, jnp.bfloat16),
            pltpu.VMEM((SPAN, widths.shape[0]), jnp.int32),
            pltpu.VMEM((widths.shape[0] + 16, TAPS), jnp.float32),
            pltpu.VMEM((widths.shape[0] + 16, TAPS), jnp.float32),
            pltpu.VMEM((2, rows, TAPS), jnp.float32),
            pltpu.VMEM((2, rows, count * BLOCK, TAPS), jnp.bfloat16),
            pltpu.VMEM((2, rows * 2 * BLOCK, count * channels), jnp.bfloat16),
            pltpu.VMEM((2, 2 * RAD * columns, count * channels), jnp.bfloat16),
            pltpu.VMEM((2, count * channels, channels), jnp.bfloat16),
            pltpu.SemaphoreType.DMA((4,)),
            pltpu.SemaphoreType.DMA((10,)),
            pltpu.SemaphoreType.DMA((10,)),
            pltpu.SemaphoreType.REGULAR,
            pltpu.SemaphoreType.REGULAR,
        ],
        compiler_params=pltpu.CompilerParams(
            collective_id=0, has_side_effects=True, vmem_limit_bytes=40 * 1024 * 1024
        ),
    )(*operands)
    results = [pltpu.with_memory_space_constraint(a, pltpu.VMEM) for a in results]
    anywhere = pl.BlockSpec(memory_space=pl.ANY)
    final = jax.ShapeDtypeStruct(fields.shape, jnp.bfloat16)
    return pl.pallas_call(
        deliver,
        out_shape=(final, final),
        in_specs=[vmem, vmem],
        out_specs=(anywhere, anywhere),
        scratch_shapes=[pltpu.SemaphoreType.DMA((2,))],
    )(*results)


def solution(mesh):
    in_specs = (P("lat", "lon", None), P("lat", "lon", None), P(), P())
    out_specs = (P("lat", "lon", None), P("lat", "lon", None))
    return jax.shard_map(body, mesh=mesh, in_specs=in_specs, out_specs=out_specs, check_vma=False)
```
